32 devices in a mesh: parts: 2 (over x), grid: 16 (over z, y, core).
Axes of the slice: x: 2, y: 2, z: 4, core: 2. Of those that a mesh axis runs over, the one named last changes fastest.
Arguments:
- field_modes: float32 [1771, 64, 256], P(None, ('parts', 'grid')), parts along dimension 1, may hold values from -6 to 6
- kl_coefficients: float32 [21, 64, 256], P(None, ('parts', 'grid')), parts along dimension 1, may hold values from 0.25 to 2
Outputs:
- applied_modes: float32 [1771, 64, 256], P(None, ('parts', 'grid')), parts along dimension 1
The draws below stay inside these ranges and needn't reach their ends.
There are 2 independent parts, one for each index of `parts`. The reference program is written for one: setup_inputs(seed, part) draws one part's arguments, and reference() takes and returns one part's arrays. A program takes and returns all parts, laid end to end along the dimension named above; each array names one. Nothing has to cross between parts.
All inputs are finite; a program needn't handle non-finite values.
Results may differ from the reference program's by a relative error of at most 0.0001.
Values sent between devices are 32-bit elements; how exact they have to be, the bound alone decides.
A program may use at most 128 MiB of HBM per device.

```python
import math
import jax
import jax.numpy as jnp
import numpy as np
from jax import lax

VARS = 20
ORDER = 3
MODES = 1771
TERMS = 21
COLS = 256
NROWS = 32


def block_levels(own_key, extent, pieces, smallest, largest):
    gain = 1.0
    for dim, shards_of in pieces:
        heights = jax.random.uniform(jax.random.fold_in(jax.random.fold_in(own_key, 6), dim), (shards_of,), jnp.float32, smallest / len(pieces), largest / len(pieces))
        gain = gain * jnp.repeat(jnp.exp(heights), extent[dim] // shards_of).reshape((-1,) + (1,) * (len(extent) - 1 - dim))
    return gain


def noise(own_key, shape, deviation, most, shards=(), kind=jnp.bfloat16):
    entries = jax.random.normal(own_key, shape, jnp.float32) * deviation
    if len(shards) > 0:
        entries = block_levels(own_key, shape, shards, -0.22, 0.18) * entries
    return jnp.clip(entries, min=-most, max=most).astype(kind)


def setup_inputs(seed: int = 0, part: int = 0) -> dict:
    key_of = jax.random.split(jax.random.key(seed), 3)
    part_keys = jax.random.split(jax.random.fold_in(key_of[2], part), 3)
    return {
        "field_modes": noise(part_keys[0], (MODES, NROWS, COLS), 1.0, 6.0, ((1, 16),), jnp.float32),
        "kl_coefficients": jnp.clip(0.25 + 1.75 * jax.random.uniform(part_keys[1], (TERMS, NROWS, COLS), jnp.float32) ** block_levels(part_keys[1], (TERMS, NROWS, COLS), ((1, 16),), -0.2, 0.2), 0.25, 2.0),
    }


def chaos_tables(nvars, order):
    levels = [[tuple([0] * nvars)]]
    for degree in range(1, order + 1):
        grown_set = set()
        for multi_index in levels[-1]:
            for variable in range(nvars):
                lifted = list(multi_index)
                lifted[variable] += 1
                grown_set.add(tuple(lifted))
        levels.append(sorted(grown_set, reverse=True))
    ordered = [multi_index for level_list in levels for multi_index in level_list]
    position = {multi_index: slot_index for slot_index, multi_index in enumerate(ordered)}
    modes_count = len(ordered)
    up_index = np.zeros((nvars, modes_count), np.int32)
    up_value = np.zeros((nvars, modes_count), np.float32)
    down_index = np.zeros((nvars, modes_count), np.int32)
    down_value = np.zeros((nvars, modes_count), np.float32)
    for slot_index, multi_index in enumerate(ordered):
        for variable in range(nvars):
            if sum(multi_index) < order:
                lifted = list(multi_index)
                lifted[variable] += 1
                up_index[variable, slot_index] = position[tuple(lifted)]
                up_value[variable, slot_index] = math.sqrt(multi_index[variable] + 1)
            if multi_index[variable] > 0:
                lowered = list(multi_index)
                lowered[variable] -= 1
                down_index[variable, slot_index] = position[tuple(lowered)]
                down_value[variable, slot_index] = math.sqrt(multi_index[variable])
    return (up_index, up_value, down_index, down_value)

def five_point(extended, conduct):
    padded = jnp.pad(extended, [(0, 0)] * (extended.ndim - 1) + [(1, 1)])
    cpadded = jnp.pad(conduct, ((0, 0), (1, 1)))
    center = padded[..., 1:-1, 1:-1]
    center_coef = cpadded[1:-1, 1:-1]
    result = jnp.zeros(center.shape, jnp.float32)
    for row_cut, col_cut in ((slice(0, -2), slice(1, -1)), (slice(2, None), slice(1, -1)), (slice(1, -1), slice(0, -2)), (slice(1, -1), slice(2, None))):
        neighbour = padded[..., row_cut, col_cut]
        neighbour_coef = cpadded[row_cut, col_cut]
        result = result + 0.5 * (center_coef + neighbour_coef) * (center - neighbour)
    return result

def reference(field_modes, kl_coefficients):
    up_index, up_value, down_index, down_value = chaos_tables(VARS, ORDER)
    up_index = jnp.asarray(up_index, jnp.int32)
    down_index = jnp.asarray(down_index, jnp.int32)
    up_value = jnp.asarray(up_value, jnp.float32)
    down_value = jnp.asarray(down_value, jnp.float32)
    padded_field = jnp.pad(field_modes, ((0, 0), (1, 1), (0, 0)))
    padded_coef = jnp.pad(kl_coefficients, ((0, 0), (1, 1), (0, 0)))
    running = five_point(padded_field, padded_coef[0])

    def add_term(variable, running):
        conduct = lax.dynamic_index_in_dim(padded_coef, variable + 1, 0, keepdims=False)
        rows_up = lax.dynamic_index_in_dim(up_index, variable, 0, keepdims=False)
        rows_down = lax.dynamic_index_in_dim(down_index, variable, 0, keepdims=False)
        scale_up = lax.dynamic_index_in_dim(up_value, variable, 0, keepdims=False)
        scale_down = lax.dynamic_index_in_dim(down_value, variable, 0, keepdims=False)
        mixed = scale_up[:, None, None] * jnp.take(padded_field, rows_up, axis=0) + scale_down[:, None, None] * jnp.take(padded_field, rows_down, axis=0)
        return running + five_point(mixed, conduct)
    return lax.fori_loop(0, VARS, add_term, running)
```

```python
import math

import jax
import jax.numpy as jnp
from jax import lax
from jax.experimental import pallas as pl
from jax.experimental.pallas import tpu as pltpu
from jax.sharding import PartitionSpec as P

VARS = 20
R2 = math.sqrt(2.0)
R6 = math.sqrt(6.0)
LANES = 128


def tri(n):
    return n * (n + 1) // 2


def idx2(i, j):
    return 1 + VARS + tri(VARS) - tri(VARS - i) + j - i


def idx3(i, j, k):
    first = 1 + VARS + tri(VARS)
    total = VARS * (VARS + 1) * (VARS + 2) // 6
    rest = VARS - i
    off = total - rest * (rest + 1) * (rest + 2) // 6
    return first + off + tri(VARS - i) - tri(VARS - j) + k - j


DEG2 = 1 + VARS
NPAIR = tri(VARS)
DEG3 = DEG2 + NPAIR
GROUP = 4


def start_low(load, w, u2, acc_a, acc_b, store):
    w0 = w(0)
    u0 = load(0)
    zero = jnp.zeros_like(u0)
    out0 = w0 * u0
    for v in range(VARS):
        out0 = out0 + w(1 + v) * load(1 + v)
    for i in range(VARS):
        for j in range(i, VARS):
            val = load(idx2(i, j))
            if i == j:
                val = val * R2
            u2[idx2(i, j) - DEG2] = val
    ones = []
    for i in range(VARS):
        total = w0 * load(1 + i) + w(1 + i) * u0
        for v in range(VARS):
            total = total + w(1 + v) * u2[idx2(min(i, v), max(i, v)) - DEG2]
        ones.append(total)
        for j in range(i, VARS):
            pos = idx2(i, j) - DEG2
            acc_a[pos] = w0 * u2[pos] + w(1 + i) * load(1 + j) + w(1 + j) * load(1 + i)
            acc_b[pos] = zero
        if i % 5 == 4:
            for n, t in enumerate(ones):
                u2[NPAIR + i - 4 + n] = t
            ones = []
    return out0


def pair_row(load, w, u2, acc_a, acc_b, store, i, j, base, b2i, same):
    w0 = w(0)
    wi = w(1 + i)
    wj = w(1 + j)
    uij = u2[b2i + j]
    total = None
    for lo in range(j, VARS, GROUP):
        ks = range(lo, min(lo + GROUP, VARS))
        u3, outs, ia, jb = [], [], [], []
        for k in ks:
            scale = (R6 if same else R2) if k == j else (R2 if same else None)
            val = load(base + (k - j))
            if scale is not None:
                val = val * scale
            wk = w(1 + k)
            out = w0 * val + wi * u2[idx2(j, k) - DEG2] + wj * u2[b2i + k] + wk * uij
            if scale is not None:
                out = out * (1.0 / scale)
            outs.append(out)
            term = wk * val
            total = term if total is None else total + term
            if k != j:
                ia.append(acc_a[b2i + k] + wj * val)
            if not same:
                jb.append(acc_b[idx2(j, k) - DEG2] + wi * val)
        for n, k in enumerate(ks):
            store(base + (k - j), outs[n])
            if k != j:
                acc_a[b2i + k] = ia.pop(0)
            if not same:
                acc_b[idx2(j, k) - DEG2] = jb.pop(0)
    acc_a[b2i + j] = acc_a[b2i + j] + total


def cubic(load, w, u2, acc_a, acc_b, store, i_lo, i_hi):
    for j in range(i_lo, VARS):
        hi = min(j, i_hi)

        def step(i, carry):
            base, b2i = carry
            pair_row(load, w, u2, acc_a, acc_b, store, i, j, base, b2i, False)
            left = VARS - 1 - i
            return base + jnp.right_shift(left * (left + 1), 1), b2i + left

        if hi > i_lo:
            lax.fori_loop(
                i_lo,
                hi,
                step,
                (jnp.int32(idx3(i_lo, j, j)), jnp.int32(idx2(i_lo, i_lo) - DEG2 - i_lo)),
            )
        if j < i_hi:
            pair_row(
                load, w, u2, acc_a, acc_b, store, j, j, idx3(j, j, j), idx2(j, j) - DEG2 - j, True
            )


def finish_low(out0, u2, acc_a, acc_b, store):
    store(0, out0)
    for i in range(VARS):
        store(1 + i, u2[NPAIR + i])
        for j in range(i, VARS):
            pos = idx2(i, j) - DEG2
            out = acc_a[pos] + acc_b[pos]
            if i == j:
                out = out * (1.0 / R2)
            store(DEG2 + pos, out)


def shifted(g):
    lane = lax.broadcasted_iota(jnp.int32, g.shape, 1)
    row = lax.broadcasted_iota(jnp.int32, g.shape, 0)
    second = (row & 2) == 2
    left = pltpu.roll(g, LANES - 1, 1)
    east = jnp.where(lane < LANES - 1, left, jnp.where(second, 0.0, pltpu.roll(left, 6, 0)))
    right = pltpu.roll(g, 1, 1)
    west = jnp.where(lane > 0, right, jnp.where(second, pltpu.roll(right, 2, 0), 0.0))
    other = jnp.where((row & 1) == 0, pltpu.roll(g, 7, 0), pltpu.roll(g, 1, 0))
    return east, west, other


def spread(first, second):
    row = lax.broadcasted_iota(jnp.int32, first.shape, 0)
    return (
        jnp.where(row < 4, first, pltpu.roll(second, 4, 0)),
        jnp.where(row < 4, pltpu.roll(first, 4, 0), second),
    )


def local_kernel(modes, f_ref, c_ref, h_ref, o_ref, u_ref, w_ref, u2, acc_a, acc_b):
    terms = 1 + VARS

    def weights(n, _):
        at = jnp.minimum(2 * n, terms - 2)
        c = c_ref[pl.ds(at, 2)].reshape(8, LANES)
        h = h_ref[pl.ds(at, 2)].reshape(8, LANES)
        east, west, other = shifted(c)
        center = 0.5 * (4.0 * c + east + west + other + h)
        a0, a1 = spread(center, -0.5 * (c + east))
        b0, b1 = spread(-0.5 * (c + west), -0.5 * (c + other))
        w_ref[0, at] = a0
        w_ref[0, at + 1] = a1
        w_ref[1, at] = b0
        w_ref[1, at + 1] = b1
        return 0

    lax.fori_loop(0, (terms + 1) // 2, weights, 0)

    def build(n, _):
        at = jnp.minimum(2 * n, modes - 2)
        g = f_ref[pl.ds(at, 2)].reshape(8, LANES)
        east, west, other = shifted(g)
        a0, a1 = spread(g, east)
        b0, b1 = spread(west, other)
        u_ref[0, at] = a0
        u_ref[0, at + 1] = a1
        u_ref[1, at] = b0
        u_ref[1, at + 1] = b1
        return 0

    lax.fori_loop(0, (modes + 1) // 2, build, 0)

    def half(n, _):
        load = lambda m: u_ref[n, m]
        w = lambda t: w_ref[n, t]

        def store(m, value):
            u_ref[n, m] = value

        out0 = start_low(load, w, u2, acc_a, acc_b, store)
        cubic(load, w, u2, acc_a, acc_b, store, 0, VARS)
        finish_low(out0, u2, acc_a, acc_b, store)
        return 0

    lax.fori_loop(0, 2, half, 0)

    def total(m, _):
        both = u_ref[0, m] + u_ref[1, m]
        o_ref[m] = both[0:4] + both[4:8]
        return 0

    lax.fori_loop(0, modes, total, 0, unroll=7)


def halo_kernel(modes, a_ref, g_ref, c_ref, h_ref, o_ref, w_ref, u2, acc_a, acc_b):
    w_ref[...] = -0.5 * (c_ref[...] + h_ref[...])
    load = lambda m: g_ref[m]
    w = lambda t: w_ref[t]

    def store(m, value):
        o_ref[m] = a_ref[m] + value

    out0 = start_low(load, w, u2, acc_a, acc_b, store)
    cubic(load, w, u2, acc_a, acc_b, store, 0, VARS)
    finish_low(out0, u2, acc_a, acc_b, store)


def tiled(array):
    n = array.shape[0]
    return array.reshape(n, 2, 2, LANES).transpose(0, 2, 1, 3).reshape(n, 4, LANES)


def exchange(array):
    size = lax.axis_size("grid")
    up = [(i, i + 1) for i in range(size - 1)]
    down = [(i + 1, i) for i in range(size - 1)]
    n = array.shape[0]
    four = array.reshape(n, 2, 2, LANES)
    above = lax.ppermute(four[:, 1], "grid", up)
    below = lax.ppermute(four[:, 0], "grid", down)
    return above, below


def merge(above, below):
    return jnp.stack([above, below], axis=2).reshape(above.shape[0], 4, LANES)


def body(field, coef):
    modes = field.shape[0]
    c4 = tiled(coef)
    f4 = tiled(field)
    hc = merge(*exchange(coef))
    above, below = exchange(field)
    params = pltpu.CompilerParams(vmem_limit_bytes=48 * 1024 * 1024)
    low = lambda s: [pltpu.VMEM((NPAIR + VARS, s, LANES), jnp.float32)] + [
        pltpu.VMEM((NPAIR, s, LANES), jnp.float32)
    ] * 2
    part = pl.pallas_call(
        lambda *refs: local_kernel(modes, *refs),
        out_shape=jax.ShapeDtypeStruct((modes, 4, LANES), jnp.float32),
        scratch_shapes=[
            pltpu.VMEM((2, modes, 8, LANES), jnp.float32),
            pltpu.VMEM((2, 1 + VARS, 8, LANES), jnp.float32),
        ]
        + low(8),
        compiler_params=params,
        cost_estimate=pl.CostEstimate(
            flops=40 * 10**6, bytes_accessed=40 * 10**6, transcendentals=0
        ),
        name="local",
    )(f4, c4, hc)
    out = pl.pallas_call(
        lambda *refs: halo_kernel(modes, *refs),
        out_shape=jax.ShapeDtypeStruct((modes, 4, LANES), jnp.float32),
        scratch_shapes=[pltpu.VMEM((1 + VARS, 4, LANES), jnp.float32)] + low(4),
        compiler_params=params,
        name="halo",
    )(part, merge(above, below), c4, hc)
    return out.reshape(modes, 2, 2, LANES).transpose(0, 2, 1, 3).reshape(field.shape)


def solution(mesh):
    placed = P(None, ("parts", "grid"), None)
    return jax.shard_map(
        body, mesh=mesh, in_specs=(placed, placed), out_specs=placed, check_vma=False
    )
```

```python
import math

import jax
import jax.numpy as jnp
from jax import lax
from jax.experimental import pallas as pl
from jax.experimental.pallas import tpu as pltpu
from jax.sharding import PartitionSpec as P

VARS = 20
R2 = math.sqrt(2.0)
R6 = math.sqrt(6.0)
LANES = 128


def tri(n):
    return n * (n + 1) // 2


def idx2(i, j):
    return 1 + VARS + tri(VARS) - tri(VARS - i) + j - i


def idx3(i, j, k):
    first = 1 + VARS + tri(VARS)
    total = VARS * (VARS + 1) * (VARS + 2) // 6
    rest = VARS - i
    off = total - rest * (rest + 1) * (rest + 2) // 6
    return first + off + tri(VARS - i) - tri(VARS - j) + k - j


DEG2 = 1 + VARS
NPAIR = tri(VARS)
DEG3 = DEG2 + NPAIR
GROUP = 4


def start_low(load, w, u2, acc_a, acc_b, store):
    w0 = w(0)
    u0 = load(0)
    zero = jnp.zeros_like(u0)
    out0 = w0 * u0
    for v in range(VARS):
        out0 = out0 + w(1 + v) * load(1 + v)
    for i in range(VARS):
        for j in range(i, VARS):
            val = load(idx2(i, j))
            if i == j:
                val = val * R2
            u2[idx2(i, j) - DEG2] = val
    ones = []
    for i in range(VARS):
        total = w0 * load(1 + i) + w(1 + i) * u0
        for v in range(VARS):
            total = total + w(1 + v) * u2[idx2(min(i, v), max(i, v)) - DEG2]
        ones.append(total)
        for j in range(i, VARS):
            pos = idx2(i, j) - DEG2
            acc_a[pos] = w0 * u2[pos] + w(1 + i) * load(1 + j) + w(1 + j) * load(1 + i)
            acc_b[pos] = zero
        if i % 5 == 4:
            for n, t in enumerate(ones):
                u2[NPAIR + i - 4 + n] = t
            ones = []
    return out0


def pair_row(load, w, u2, acc_a, acc_b, store, i, j, base, b2i, same):
    w0 = w(0)
    wi = w(1 + i)
    wj = w(1 + j)
    uij = u2[b2i + j]
    total = None
    for lo in range(j, VARS, GROUP):
        ks = range(lo, min(lo + GROUP, VARS))
        u3, outs, ia, jb = [], [], [], []
        for k in ks:
            scale = (R6 if same else R2) if k == j else (R2 if same else None)
            val = load(base + (k - j))
            if scale is not None:
                val = val * scale
            wk = w(1 + k)
            out = w0 * val + wi * u2[idx2(j, k) - DEG2] + wj * u2[b2i + k] + wk * uij
            if scale is not None:
                out = out * (1.0 / scale)
            outs.append(out)
            term = wk * val
            total = term if total is None else total + term
            if k != j:
                ia.append(acc_a[b2i + k] + wj * val)
            if not same:
                jb.append(acc_b[idx2(j, k) - DEG2] + wi * val)
        for n, k in enumerate(ks):
            store(base + (k - j), outs[n])
            if k != j:
                acc_a[b2i + k] = ia.pop(0)
            if not same:
                acc_b[idx2(j, k) - DEG2] = jb.pop(0)
    acc_a[b2i + j] = acc_a[b2i + j] + total


def cubic(load, w, u2, acc_a, acc_b, store, i_lo, i_hi):
    for j in range(i_lo, VARS):
        hi = min(j, i_hi)

        def step(i, carry):
            base, b2i = carry
            pair_row(load, w, u2, acc_a, acc_b, store, i, j, base, b2i, False)
            left = VARS - 1 - i
            return base + jnp.right_shift(left * (left + 1), 1), b2i + left

        if hi > i_lo:
            lax.fori_loop(
                i_lo,
                hi,
                step,
                (jnp.int32(idx3(i_lo, j, j)), jnp.int32(idx2(i_lo, i_lo) - DEG2 - i_lo)),
            )
        if j < i_hi:
            pair_row(
                load, w, u2, acc_a, acc_b, store, j, j, idx3(j, j, j), idx2(j, j) - DEG2 - j, True
            )


def finish_low(out0, u2, acc_a, acc_b, store):
    store(0, out0)
    for i in range(VARS):
        store(1 + i, u2[NPAIR + i])
        for j in range(i, VARS):
            pos = idx2(i, j) - DEG2
            out = acc_a[pos] + acc_b[pos]
            if i == j:
                out = out * (1.0 / R2)
            store(DEG2 + pos, out)


def shifted(g):
    lane = lax.broadcasted_iota(jnp.int32, g.shape, 1)
    row = lax.broadcasted_iota(jnp.int32, g.shape, 0)
    second = (row & 2) == 2
    left = pltpu.roll(g, LANES - 1, 1)
    east = jnp.where(lane < LANES - 1, left, jnp.where(second, 0.0, pltpu.roll(left, 6, 0)))
    right = pltpu.roll(g, 1, 1)
    west = jnp.where(lane > 0, right, jnp.where(second, pltpu.roll(right, 2, 0), 0.0))
    other = jnp.where((row & 1) == 0, pltpu.roll(g, 7, 0), pltpu.roll(g, 1, 0))
    return east, west, other


def spread(first, second):
    row = lax.broadcasted_iota(jnp.int32, first.shape, 0)
    return (
        jnp.where(row < 4, first, pltpu.roll(second, 4, 0)),
        jnp.where(row < 4, pltpu.roll(first, 4, 0), second),
    )


TERMS = 1 + VARS
SLOTS = 24
COEF = 4 * SLOTS
BUILD = 8
FIRST_VARS = (0, 2, 5, 9, VARS)


def rounded(n, to):
    return -(-n // to) * to


def blocks(lo, hi, width, step):
    groups = (hi - lo) // width
    if groups > 0:
        lax.fori_loop(0, groups, lambda n, c: (step(lo + n * width, width), c)[1], 0)
    for n in range(lo + groups * width, hi):
        step(n, 1)


def fused_kernel(
    modes, devices, f_ref, c_ref, o_ref,
    rows, top, bottom, above, below, send_sem, recv_sem, u_ref, w_ref, d_ref, wh_ref,
    u2, acc_a, acc_b, h2, hacc_a, hacc_b,
):
    me = lax.axis_index("grid")
    has_up = me > 0
    has_down = me < devices - 1
    mesh_id = pl.DeviceIdType.MESH
    barrier = pltpu.get_barrier_semaphore()

    @pl.when(has_up)
    def _():
        pl.semaphore_signal(barrier, inc=1, device_id={"grid": me - 1}, device_id_type=mesh_id)

    @pl.when(has_down)
    def _():
        pl.semaphore_signal(barrier, inc=1, device_id={"grid": me + 1}, device_id_type=mesh_id)

    total_rows = rows.shape[0]
    cuts = [0]
    for i in FIRST_VARS[1:-1]:
        cuts.append(rounded(2 * SLOTS + 2 * idx3(i, i, i), 8))
    cuts.append(total_rows // 2)

    def copies(n):
        part = pl.ds(cuts[n], cuts[n + 1] - cuts[n])
        going_up = pltpu.make_async_remote_copy(
            src_ref=top.at[part], dst_ref=below.at[part],
            send_sem=send_sem.at[0, n], recv_sem=recv_sem.at[0, n],
            device_id={"grid": me - 1}, device_id_type=mesh_id,
        )
        going_down = pltpu.make_async_remote_copy(
            src_ref=bottom.at[part], dst_ref=above.at[part],
            send_sem=send_sem.at[1, n], recv_sem=recv_sem.at[1, n],
            device_id={"grid": me + 1}, device_id_type=mesh_id,
        )
        return going_up, going_down

    rows[0 : 4 * TERMS] = c_ref[...].reshape(4 * TERMS, LANES)
    rows[4 * TERMS : COEF] = jnp.zeros((COEF - 4 * TERMS, LANES), jnp.float32)

    def fill(n, count):
        value = f_ref[pl.ds(4 * n, 4 * count)].reshape(16 * count, LANES)
        rows[pl.ds(pl.multiple_of(COEF + 16 * n, 16), 16 * count)] = value

    def pack(n, count):
        for q in range(count):
            at = 16 * (n + q)
            low = rows[pl.ds(at, 8, stride=2)]
            high = rows[pl.ds(at + 1, 8, stride=2)]
            to = pl.ds(pl.multiple_of(8 * (n + q), 8), 8)
            top[to] = low
            bottom[to] = high

    whole = modes // 4
    done = 0
    for n in range(len(cuts) - 1):
        until = (cuts[n + 1] - 2 * SLOTS) // 8
        blocks(done, min(until, whole), 4, fill)
        if until > whole:
            left = modes - 4 * whole
            at = COEF + 16 * whole
            rows[at : at + 4 * left] = f_ref[4 * whole : modes].reshape(4 * left, LANES)
            rows[at + 4 * left : total_rows] = jnp.zeros(
                (total_rows - at - 4 * left, LANES), jnp.float32
            )
        done = until
        blocks(cuts[n] // 8, cuts[n + 1] // 8, 8, pack)
        going_up, going_down = copies(n)
        if n == 0:
            pl.semaphore_wait(barrier, has_up.astype(jnp.int32) + has_down.astype(jnp.int32))

        @pl.when(has_up)
        def _():
            going_up.start()

        @pl.when(has_down)
        def _():
            going_down.start()

    def weights(n, _):
        c = rows[pl.ds(pl.multiple_of(8 * n, 8), 8)]
        east, west, other = shifted(c)
        a0, a1 = spread(0.5 * (3.0 * c + east + west + other), -0.5 * (c + east))
        b0, b1 = spread(-0.5 * (c + west), -0.5 * (c + other))
        w_ref[0, 2 * n] = a0
        w_ref[0, 2 * n + 1] = a1
        w_ref[1, 2 * n] = b0
        w_ref[1, 2 * n + 1] = b1
        return 0

    lax.fori_loop(0, (TERMS + 1) // 2, weights, 0)

    def build(n, count):
        made = []
        for q in range(count):
            g = rows[pl.ds(pl.multiple_of(COEF + 8 * (n + q), 8), 8)]
            east, west, other = shifted(g)
            made.append(spread(g, east) + spread(west, other))
        for q in range(count):
            a0, a1, b0, b1 = made[q]
            at = 2 * (n + q)
            u_ref[0, at] = a0
            u_ref[0, at + 1] = a1
            u_ref[1, at] = b0
            u_ref[1, at + 1] = b1

    blocks(0, (modes + 1) // 2, BUILD, build)

    def half(n, _):
        load = lambda m: u_ref[n, m]
        w = lambda t: w_ref[n, t]

        def store(m, value):
            u_ref[n, m] = value

        out0 = start_low(load, w, u2, acc_a, acc_b, store)
        cubic(load, w, u2, acc_a, acc_b, store, 0, VARS)
        finish_low(out0, u2, acc_a, acc_b, store)
        return 0

    lax.fori_loop(0, 2, half, 0)

    def total(n, count):
        made = []
        for q in range(count):
            both = u_ref[0, n + q] + u_ref[1, n + q]
            made.append(both[0:4] + both[4:8])
        for q in range(count):
            o_ref[n + q] = made[q]

    blocks(0, modes, 8, total)

    @pl.when(jnp.logical_not(has_up))
    def _():
        above[...] = jnp.zeros_like(above)

    @pl.when(jnp.logical_not(has_down))
    def _():
        below[...] = jnp.zeros_like(below)

    def differ(n, count):
        made = []
        for q in range(count):
            at = 16 * (n + q)
            of = pl.ds(pl.multiple_of(8 * (n + q), 8), 8)
            made.append(
                (rows[pl.ds(at, 8, stride=2)] - above[of], rows[pl.ds(at + 1, 8, stride=2)] - below[of])
            )
        for q in range(count):
            at = 16 * (n + q)
            rows[pl.ds(at, 8, stride=2)] = made[q][0]
            rows[pl.ds(at + 1, 8, stride=2)] = made[q][1]

    def unfold(n, count):
        value = rows[pl.ds(pl.multiple_of(COEF + 16 * n, 16), 16 * count)]
        d_ref[pl.ds(4 * n, 4 * count)] = value.reshape(4 * count, 4, LANES)

    load = lambda m: d_ref[m]
    w = lambda t: wh_ref[t]

    def store(m, value):
        o_ref[m] = o_ref[m] + value

    out0 = None
    for n in range(len(cuts) - 1):
        going_up, going_down = copies(n)

        @pl.when(has_down)
        def _():
            going_up.wait_recv()

        @pl.when(has_up)
        def _():
            going_down.wait_recv()

        blocks(cuts[n] // 8, cuts[n + 1] // 8, 8, differ)
        blocks(max(cuts[n] - 2 * SLOTS, 0) // 8, (cuts[n + 1] - 2 * SLOTS) // 8, 4, unfold)
        if n == 0:
            change = rows[0 : 4 * TERMS].reshape(TERMS, 4, LANES)
            wh_ref[...] = c_ref[...] - 0.5 * change
            out0 = start_low(load, w, h2, hacc_a, hacc_b, store)
        cubic(load, w, h2, hacc_a, hacc_b, store, FIRST_VARS[n], FIRST_VARS[n + 1])
    finish_low(out0, h2, hacc_a, hacc_b, store)

    for n in range(len(cuts) - 1):
        going_up, going_down = copies(n)

        @pl.when(has_up)
        def _():
            going_up.wait_send()

        @pl.when(has_down)
        def _():
            going_down.wait_send()


def tiled(array):
    n = array.shape[0]
    return array.reshape(n, 2, 2, LANES).transpose(0, 2, 1, 3).reshape(n, 4, LANES)


def body(devices, field, coef):
    modes = field.shape[0]
    even = rounded(modes, 4)
    total_rows = COEF + 4 * even
    chunks = len(FIRST_VARS) - 1
    buf = lambda *shape: pltpu.VMEM(shape + (LANES,), jnp.float32)
    low = lambda s: [buf(NPAIR + VARS, s), buf(NPAIR, s), buf(NPAIR, s)]
    out = pl.pallas_call(
        lambda *refs: fused_kernel(modes, devices, *refs),
        out_shape=jax.ShapeDtypeStruct((modes, 4, LANES), jnp.float32),
        in_specs=[pl.BlockSpec(memory_space=pltpu.VMEM)] * 2,
        out_specs=pl.BlockSpec(memory_space=pltpu.VMEM),
        scratch_shapes=[buf(total_rows)]
        + [buf(total_rows // 2)] * 4
        + [pltpu.SemaphoreType.DMA((2, chunks))] * 2
        + [buf(2, even, 8), buf(2, TERMS + 1, 8), buf(even, 4), buf(TERMS, 4)]
        + low(8)
        + low(4),
        compiler_params=pltpu.CompilerParams(
            collective_id=0, has_side_effects=True, vmem_limit_bytes=56 * 1024 * 1024
        ),
        name="fused",
    )(tiled(field), tiled(coef))
    return out.reshape(modes, 2, 2, LANES).transpose(0, 2, 1, 3).reshape(field.shape)


def solution(mesh):
    placed = P(None, ("parts", "grid"), None)
    devices = mesh.shape["grid"]
    return jax.shard_map(
        lambda field, coef: body(devices, field, coef),
        mesh=mesh,
        in_specs=(placed, placed),
        out_specs=placed,
        check_vma=False,
    )
```

```python
import math

import jax
import jax.numpy as jnp
from jax import lax
from jax.experimental import pallas as pl
from jax.experimental.pallas import tpu as pltpu
from jax.sharding import PartitionSpec as P

VARS = 20
R2 = math.sqrt(2.0)
R6 = math.sqrt(6.0)
LANES = 128


def tri(n):
    return n * (n + 1) // 2


def idx2(i, j):
    return 1 + VARS + tri(VARS) - tri(VARS - i) + j - i


def idx3(i, j, k):
    first = 1 + VARS + tri(VARS)
    total = VARS * (VARS + 1) * (VARS + 2) // 6
    rest = VARS - i
    off = total - rest * (rest + 1) * (rest + 2) // 6
    return first + off + tri(VARS - i) - tri(VARS - j) + k - j


DEG2 = 1 + VARS
NPAIR = tri(VARS)
DEG3 = DEG2 + NPAIR
GROUP = 4


def start_low(load, w, u2, acc_a, acc_b, store):
    w0 = w(0)
    u0 = load(0)
    zero = jnp.zeros_like(u0)
    out0 = w0 * u0
    for v in range(VARS):
        out0 = out0 + w(1 + v) * load(1 + v)
    for i in range(VARS):
        for j in range(i, VARS):
            val = load(idx2(i, j))
            if i == j:
                val = val * R2
            u2[idx2(i, j) - DEG2] = val
    ones = []
    for i in range(VARS):
        total = w0 * load(1 + i) + w(1 + i) * u0
        for v in range(VARS):
            total = total + w(1 + v) * u2[idx2(min(i, v), max(i, v)) - DEG2]
        ones.append(total)
        for j in range(i, VARS):
            pos = idx2(i, j) - DEG2
            acc_a[pos] = w0 * u2[pos] + w(1 + i) * load(1 + j) + w(1 + j) * load(1 + i)
            acc_b[pos] = zero
        if i % 5 == 4:
            for n, t in enumerate(ones):
                u2[NPAIR + i - 4 + n] = t
            ones = []
    return out0


def pair_row(load, w, u2, acc_a, acc_b, store, i, j, base, b2i, same):
    w0 = w(0)
    wi = w(1 + i)
    wj = w(1 + j)
    uij = u2[b2i + j]
    total = None
    for lo in range(j, VARS, GROUP):
        ks = range(lo, min(lo + GROUP, VARS))
        u3, outs, ia, jb = [], [], [], []
        for k in ks:
            scale = (R6 if same else R2) if k == j else (R2 if same else None)
            val = load(base + (k - j))
            if scale is not None:
                val = val * scale
            wk = w(1 + k)
            out = w0 * val + wi * u2[idx2(j, k) - DEG2] + wj * u2[b2i + k] + wk * uij
            if scale is not None:
                out = out * (1.0 / scale)
            outs.append(out)
            term = wk * val
            total = term if total is None else total + term
            if k != j:
                ia.append(acc_a[b2i + k] + wj * val)
            if not same:
                jb.append(acc_b[idx2(j, k) - DEG2] + wi * val)
        for n, k in enumerate(ks):
            store(base + (k - j), outs[n])
            if k != j:
                acc_a[b2i + k] = ia.pop(0)
            if not same:
                acc_b[idx2(j, k) - DEG2] = jb.pop(0)
    acc_a[b2i + j] = acc_a[b2i + j] + total


def cubic(load, w, u2, acc_a, acc_b, store, i_lo, i_hi):
    for j in range(i_lo, VARS):
        hi = min(j, i_hi)

        def step(i, carry):
            base, b2i = carry
            pair_row(load, w, u2, acc_a, acc_b, store, i, j, base, b2i, False)
            left = VARS - 1 - i
            return base + jnp.right_shift(left * (left + 1), 1), b2i + left

        if hi > i_lo:
            lax.fori_loop(
                i_lo,
                hi,
                step,
                (jnp.int32(idx3(i_lo, j, j)), jnp.int32(idx2(i_lo, i_lo) - DEG2 - i_lo)),
            )
        if j < i_hi:
            pair_row(
                load, w, u2, acc_a, acc_b, store, j, j, idx3(j, j, j), idx2(j, j) - DEG2 - j, True
            )


def finish_low(out0, u2, acc_a, acc_b, store):
    store(0, out0)
    for i in range(VARS):
        store(1 + i, u2[NPAIR + i])
        for j in range(i, VARS):
            pos = idx2(i, j) - DEG2
            out = acc_a[pos] + acc_b[pos]
            if i == j:
                out = out * (1.0 / R2)
            store(DEG2 + pos, out)


def shifted(g):
    lane = lax.broadcasted_iota(jnp.int32, g.shape, 1)
    row = lax.broadcasted_iota(jnp.int32, g.shape, 0)
    second = (row & 2) == 2
    left = pltpu.roll(g, LANES - 1, 1)
    east = jnp.where(lane < LANES - 1, left, jnp.where(second, 0.0, pltpu.roll(left, 6, 0)))
    right = pltpu.roll(g, 1, 1)
    west = jnp.where(lane > 0, right, jnp.where(second, pltpu.roll(right, 2, 0), 0.0))
    other = jnp.where((row & 1) == 0, pltpu.roll(g, 7, 0), pltpu.roll(g, 1, 0))
    return east, west, other


def spread(first, second):
    row = lax.broadcasted_iota(jnp.int32, first.shape, 0)
    return (
        jnp.where(row < 4, first, pltpu.roll(second, 4, 0)),
        jnp.where(row < 4, pltpu.roll(first, 4, 0), second),
    )


TERMS = 1 + VARS
SLOTS = 24
COEF = 4 * SLOTS
BUILD = 8
FIRST_VARS = (0, 1, 3, 6, 11, VARS)


def rounded(n, to):
    return -(-n // to) * to


def blocks(lo, hi, width, step):
    groups = (hi - lo) // width
    if groups > 0:
        lax.fori_loop(0, groups, lambda n, c: (step(lo + n * width, width), c)[1], 0)
    for n in range(lo + groups * width, hi):
        step(n, 1)


def fused_kernel(
    modes, devices, f_ref, c_ref, o_ref,
    rows, top, bottom, above, below, send_sem, recv_sem, u_ref, w_ref, d_ref, wh_ref,
    u2, acc_a, acc_b, h2, hacc_a, hacc_b,
):
    me = lax.axis_index("grid")
    has_up = me > 0
    has_down = me < devices - 1
    mesh_id = pl.DeviceIdType.MESH
    barrier = pltpu.get_barrier_semaphore()

    @pl.when(has_up)
    def _():
        pl.semaphore_signal(barrier, inc=1, device_id={"grid": me - 1}, device_id_type=mesh_id)

    @pl.when(has_down)
    def _():
        pl.semaphore_signal(barrier, inc=1, device_id={"grid": me + 1}, device_id_type=mesh_id)

    total_rows = rows.shape[0]
    cuts = [0]
    for i in FIRST_VARS[1:-1]:
        cuts.append(rounded(2 * SLOTS + 2 * idx3(i, i, i), 8))
    cuts.append(total_rows // 2)

    def copies(n):
        part = pl.ds(cuts[n], cuts[n + 1] - cuts[n])
        going_up = pltpu.make_async_remote_copy(
            src_ref=top.at[part], dst_ref=below.at[part],
            send_sem=send_sem.at[0, n], recv_sem=recv_sem.at[0, n],
            device_id={"grid": me - 1}, device_id_type=mesh_id,
        )
        going_down = pltpu.make_async_remote_copy(
            src_ref=bottom.at[part], dst_ref=above.at[part],
            send_sem=send_sem.at[1, n], recv_sem=recv_sem.at[1, n],
            device_id={"grid": me + 1}, device_id_type=mesh_id,
        )
        return going_up, going_down

    rows[0 : 4 * TERMS] = c_ref[...].reshape(4 * TERMS, LANES)
    rows[4 * TERMS : COEF] = jnp.zeros((COEF - 4 * TERMS, LANES), jnp.float32)

    def fill(n, count):
        value = f_ref[pl.ds(4 * n, 4 * count)].reshape(16 * count, LANES)
        rows[pl.ds(pl.multiple_of(COEF + 16 * n, 16), 16 * count)] = value

    def pack(n, count):
        for q in range(count):
            at = 16 * (n + q)
            low = rows[pl.ds(at, 8, stride=2)]
            high = rows[pl.ds(at + 1, 8, stride=2)]
            to = pl.ds(pl.multiple_of(8 * (n + q), 8), 8)
            top[to] = low
            bottom[to] = high

    whole = modes // 4
    done = 0
    for n in range(len(cuts) - 1):
        until = (cuts[n + 1] - 2 * SLOTS) // 8
        blocks(done, min(until, whole), 4, fill)
        if until > whole:
            left = modes - 4 * whole
            at = COEF + 16 * whole
            rows[at : at + 4 * left] = f_ref[4 * whole : modes].reshape(4 * left, LANES)
            rows[at + 4 * left : total_rows] = jnp.zeros(
                (total_rows - at - 4 * left, LANES), jnp.float32
            )
        done = until
        blocks(cuts[n] // 8, cuts[n + 1] // 8, 8, pack)
        going_up, going_down = copies(n)
        if n == 0:
            pl.semaphore_wait(barrier, has_up.astype(jnp.int32) + has_down.astype(jnp.int32))

        @pl.when(has_up)
        def _():
            going_up.start()

        @pl.when(has_down)
        def _():
            going_down.start()

    def weights(n, _):
        c = rows[pl.ds(pl.multiple_of(8 * n, 8), 8)]
        east, west, other = shifted(c)
        a0, a1 = spread(0.5 * (3.0 * c + east + west + other), -0.5 * (c + east))
        b0, b1 = spread(-0.5 * (c + west), -0.5 * (c + other))
        w_ref[0, 2 * n] = a0
        w_ref[0, 2 * n + 1] = a1
        w_ref[1, 2 * n] = b0
        w_ref[1, 2 * n + 1] = b1
        return 0

    lax.fori_loop(0, (TERMS + 1) // 2, weights, 0)

    def build(n, count):
        made = []
        for q in range(count):
            g = rows[pl.ds(pl.multiple_of(COEF + 8 * (n + q), 8), 8)]
            east, west, other = shifted(g)
            made.append(spread(g, east) + spread(west, other))
        for q in range(count):
            a0, a1, b0, b1 = made[q]
            at = 2 * (n + q)
            u_ref[0, at] = a0
            u_ref[0, at + 1] = a1
            u_ref[1, at] = b0
            u_ref[1, at + 1] = b1

    blocks(0, (modes + 1) // 2, BUILD, build)

    def half(n, _):
        load = lambda m: u_ref[n, m]
        w = lambda t: w_ref[n, t]

        def store(m, value):
            u_ref[n, m] = value

        out0 = start_low(load, w, u2, acc_a, acc_b, store)
        cubic(load, w, u2, acc_a, acc_b, store, 0, VARS)
        finish_low(out0, u2, acc_a, acc_b, store)
        return 0

    lax.fori_loop(0, 2, half, 0)

    def total(n, count):
        made = []
        for q in range(count):
            both = u_ref[0, n + q] + u_ref[1, n + q]
            made.append(both[0:4] + both[4:8])
        for q in range(count):
            o_ref[n + q] = made[q]

    blocks(0, modes, 8, total)

    @pl.when(jnp.logical_not(has_up))
    def _():
        above[...] = jnp.zeros_like(above)

    @pl.when(jnp.logical_not(has_down))
    def _():
        below[...] = jnp.zeros_like(below)

    def differ(n, count):
        made = []
        for q in range(count):
            at = 16 * (n + q)
            of = pl.ds(pl.multiple_of(8 * (n + q), 8), 8)
            made.append(
                (rows[pl.ds(at, 8, stride=2)] - above[of], rows[pl.ds(at + 1, 8, stride=2)] - below[of])
            )
        for q in range(count):
            at = 16 * (n + q)
            rows[pl.ds(at, 8, stride=2)] = made[q][0]
            rows[pl.ds(at + 1, 8, stride=2)] = made[q][1]

    def unfold(n, count):
        value = rows[pl.ds(pl.multiple_of(COEF + 16 * n, 16), 16 * count)]
        d_ref[pl.ds(4 * n, 4 * count)] = value.reshape(4 * count, 4, LANES)

    load = lambda m: d_ref[m]
    w = lambda t: wh_ref[t]

    def store(m, value):
        o_ref[m] = o_ref[m] + value

    out0 = None
    for n in range(len(cuts) - 1):
        going_up, going_down = copies(n)

        @pl.when(has_down)
        def _():
            going_up.wait_recv()

        @pl.when(has_up)
        def _():
            going_down.wait_recv()

        blocks(cuts[n] // 8, cuts[n + 1] // 8, 8, differ)
        blocks(max(cuts[n] - 2 * SLOTS, 0) // 8, (cuts[n + 1] - 2 * SLOTS) // 8, 4, unfold)
        if n == 0:
            change = rows[0 : 4 * TERMS].reshape(TERMS, 4, LANES)
            wh_ref[...] = c_ref[...] - 0.5 * change
            out0 = start_low(load, w, h2, hacc_a, hacc_b, store)
        cubic(load, w, h2, hacc_a, hacc_b, store, FIRST_VARS[n], FIRST_VARS[n + 1])
    finish_low(out0, h2, hacc_a, hacc_b, store)

    for n in range(len(cuts) - 1):
        going_up, going_down = copies(n)

        @pl.when(has_up)
        def _():
            going_up.wait_send()

        @pl.when(has_down)
        def _():
            going_down.wait_send()


def tiled(array):
    n = array.shape[0]
    return array.reshape(n, 2, 2, LANES).transpose(0, 2, 1, 3).reshape(n, 4, LANES)


def body(devices, field, coef):
    modes = field.shape[0]
    even = rounded(modes, 4)
    total_rows = COEF + 4 * even
    chunks = len(FIRST_VARS) - 1
    buf = lambda *shape: pltpu.VMEM(shape + (LANES,), jnp.float32)
    low = lambda s: [buf(NPAIR + VARS, s), buf(NPAIR, s), buf(NPAIR, s)]
    out = pl.pallas_call(
        lambda *refs: fused_kernel(modes, devices, *refs),
        out_shape=jax.ShapeDtypeStruct((modes, 4, LANES), jnp.float32),
        in_specs=[pl.BlockSpec(memory_space=pltpu.VMEM)] * 2,
        out_specs=pl.BlockSpec(memory_space=pltpu.VMEM),
        scratch_shapes=[buf(total_rows)]
        + [buf(total_rows // 2)] * 4
        + [pltpu.SemaphoreType.DMA((2, chunks))] * 2
        + [buf(2, even, 8), buf(2, TERMS + 1, 8), buf(even, 4), buf(TERMS, 4)]
        + low(8)
        + low(4),
        compiler_params=pltpu.CompilerParams(
            collective_id=0, has_side_effects=True, vmem_limit_bytes=46 * 1024 * 1024
        ),
        name="fused",
    )(tiled(field), tiled(coef))
    return out.reshape(modes, 2, 2, LANES).transpose(0, 2, 1, 3).reshape(field.shape)


def solution(mesh):
    placed = P(None, ("parts", "grid"), None)
    devices = mesh.shape["grid"]
    return jax.shard_map(
        lambda field, coef: body(devices, field, coef),
        mesh=mesh,
        in_specs=(placed, placed),
        out_specs=placed,
        check_vma=False,
    )
```
